32 devices in a mesh: row: 4 (over y, core), col: 8 (over z, x).
Axes of the slice: x: 2, y: 2, z: 4, core: 2. Of those that a mesh axis runs over, the one named last changes fastest.
Arguments:
- transmission: float32 [2, 2, 2048, 2048], P(None, None, 'row', 'col'), may hold values from -5 to 5
- probe_field: float32 [2, 256, 256], replicated, may hold values from -6 to 6
- prop_phase: float32 [256, 256], replicated, may hold values from -3.140625 to 3.140625
- amplitude: float32 [4, 8, 4, 256, 256], P('row', 'col'), may hold values from 0 to 2
- window_count: int32 [4, 8], P('row', 'col'), may hold values from 1 to 4
- offset_row: int32 [4, 8, 4], P('row', 'col'), may hold values from 0 to 384
- offset_col: int32 [4, 8, 4], P('row', 'col'), may hold values from 0 to 128
- window_batch: int32 [4, 8, 4], P('row', 'col'), may hold values from 0 to 2
Outputs:
- updated: float32 [2, 2, 2048, 2048], P(None, None, 'row', 'col')
The draws below stay inside these ranges and needn't reach their ends.
All inputs are finite; a program needn't handle non-finite values.
Results may differ from the reference program's by a relative error of at most 0.0003.
Values sent between devices are 32-bit elements; how exact they have to be, the bound alone decides.
A program may use at most 64 MiB of HBM per device.

```python
import jax
import jax.numpy as jnp
from jax import lax

WIN = 256
STRIP = 128
TILE_R = 512
TILE_C = 256
SLOTS = 4
BATCHES = 3
TROWS = 4
TCOLS = 8
OBJ_R = 2048
OBJ_C = 2048
N_ROW = 4
N_COL = 8


def set_ends(drawn, key, smallest, top_value):
    dims = drawn.shape
    spot = [jax.random.randint(jax.random.fold_in(key, axis), (), 0, dims[axis]) for axis in range(len(dims))]
    drawn = drawn.at[tuple(spot)].set(smallest)
    longest = dims.index(max(dims))
    spot[longest] = (spot[longest] + 1) % dims[longest]
    return drawn.at[tuple(spot)].set(top_value)


def steps_of(own_key, extent, pieces, least, top_value):
    gain, own = 1.0, jax.random.fold_in(own_key, 6)
    for dim, blocks in pieces:
        heights = jnp.exp(jax.random.uniform(jax.random.fold_in(own, dim), (blocks,), jnp.float32, least / len(pieces), top_value / len(pieces)))
        gain = gain * jnp.repeat(heights, extent[dim] // blocks).reshape([-1 if axis == dim else 1 for axis in range(len(extent))])
    return gain


def bell_draw(own_key, dims, spread, most, cuts=(), kind=jnp.bfloat16):
    values = jax.random.normal(own_key, dims, jnp.float32) * spread
    if len(cuts) > 0:
        values = steps_of(own_key, dims, cuts, -0.22, 0.18) * values
    return jnp.clip(values, min=-most, max=most).astype(kind)


def setup_inputs(seed: int = 0) -> dict:
    streams_of = jax.random.split(jax.random.key(seed), 9)
    return {
        "transmission": bell_draw(streams_of[0], (2, 2, OBJ_R, OBJ_C), 0.7, 5.0, ((2, 4), (3, 8)), jnp.float32),
        "probe_field": bell_draw(streams_of[1], (2, WIN, WIN), 1.0, 6.0, (), jnp.float32),
        "prop_phase": jnp.clip(jax.random.uniform(streams_of[2], (WIN, WIN), jnp.float32, -3.140625, 3.140625), -3.140625, 3.140625),
        "amplitude": jnp.clip(2.0 * jax.random.uniform(streams_of[3], (TROWS, TCOLS, SLOTS, WIN, WIN), jnp.float32) ** steps_of(streams_of[3], (TROWS, TCOLS, SLOTS, WIN, WIN), ((0, 4), (1, 8)), -0.2, 0.2), 0.0, 2.0),
        "window_count": set_ends(jax.random.randint(streams_of[4], (TROWS, TCOLS), 1, SLOTS + 1), jax.random.fold_in(streams_of[4], 1), 1, SLOTS).astype(jnp.int32),
        "offset_row": set_ends(jax.random.randint(streams_of[5], (TROWS, TCOLS, SLOTS), 0, TILE_R - STRIP + 1), jax.random.fold_in(streams_of[5], 1), 0, TILE_R - STRIP).astype(jnp.int32),
        "offset_col": set_ends(jax.random.randint(streams_of[6], (TROWS, TCOLS, SLOTS), 0, TILE_C - STRIP + 1), jax.random.fold_in(streams_of[6], 1), 0, TILE_C - STRIP).astype(jnp.int32),
        "window_batch": set_ends(jax.random.randint(streams_of[7], (TROWS, TCOLS, SLOTS), 0, BATCHES), jax.random.fold_in(streams_of[7], 1), 0, BATCHES - 1).astype(jnp.int32),
    }


step_rate = 0.5


def forward_two(field):
    return jnp.fft.fft2(field, norm="ortho")


def inverse_two(field):
    return jnp.fft.ifft2(field, norm="ortho")


def window_terms(piece_one, piece_two, probe_c, propagator, measured):
    psi_one = probe_c * piece_one
    between = inverse_two(propagator * forward_two(psi_one))
    far = forward_two(between * piece_two)
    magnitude = jnp.abs(far)
    chi = far * (1.0 - measured / jnp.maximum(magnitude, 1.0))
    back_two = inverse_two(chi)
    grad_two = jnp.conj(between) * back_two
    back_mid = jnp.conj(piece_two) * back_two
    back_one = inverse_two(jnp.conj(propagator) * forward_two(back_mid))
    grad_one = jnp.conj(probe_c) * back_one
    return grad_one, grad_two


def reference(transmission, probe_field, prop_phase, amplitude, window_count, offset_row, offset_col, window_batch):
    slice_one = transmission[0, 0] + 1j * transmission[0, 1]
    slice_two = transmission[1, 0] + 1j * transmission[1, 1]
    probe_c = probe_field[0] + 1j * probe_field[1]
    propagator = jnp.cos(prop_phase) + 1j * jnp.sin(prop_phase)
    tile_rows = (jnp.arange(N_ROW, dtype=jnp.int32) * TILE_R)[:, None, None]
    tile_cols = (jnp.arange(N_COL, dtype=jnp.int32) * TILE_C)[None, :, None]
    glob_row = (tile_rows + offset_row).reshape(-1).astype(jnp.int32)
    glob_col = (tile_cols + offset_col).reshape(-1).astype(jnp.int32)
    slot_ids = jnp.arange(SLOTS, dtype=jnp.int32)[None, None, :]
    in_use = (slot_ids < window_count[:, :, None]).reshape(-1)
    batches = window_batch.reshape(-1)
    measured_all = amplitude.reshape(-1, WIN, WIN)
    for batch in range(BATCHES):
        padded_one = jnp.pad(slice_one, ((0, STRIP), (0, STRIP)))
        padded_two = jnp.pad(slice_two, ((0, STRIP), (0, STRIP)))
        weights = jnp.where(in_use & (batches == batch), 1.0, 0.0).astype(jnp.float32)

        def visit(carry, item):
            accum_one, accum_two = carry
            row_at, col_at, weight, measured = item
            piece_one = lax.dynamic_slice(padded_one, (row_at, col_at), (WIN, WIN))
            piece_two = lax.dynamic_slice(padded_two, (row_at, col_at), (WIN, WIN))
            grad_one, grad_two = window_terms(piece_one, piece_two, probe_c, propagator, measured)
            old_one = lax.dynamic_slice(accum_one, (row_at, col_at), (WIN, WIN))
            old_two = lax.dynamic_slice(accum_two, (row_at, col_at), (WIN, WIN))
            accum_one = lax.dynamic_update_slice(accum_one, old_one + weight * grad_one, (row_at, col_at))
            accum_two = lax.dynamic_update_slice(accum_two, old_two + weight * grad_two, (row_at, col_at))
            return (accum_one, accum_two), None

        start = (jnp.zeros_like(padded_one), jnp.zeros_like(padded_two))
        (accum_one, accum_two), _ = lax.scan(visit, start, (glob_row, glob_col, weights, measured_all))
        slice_one = slice_one - step_rate * accum_one[:OBJ_R, :OBJ_C]
        slice_two = slice_two - step_rate * accum_two[:OBJ_R, :OBJ_C]
    result = jnp.stack([jnp.stack([jnp.real(slice_one), jnp.imag(slice_one)]),
                        jnp.stack([jnp.real(slice_two), jnp.imag(slice_two)])])
    return result.astype(jnp.float32)
```

```python
import functools
import math

import jax
import jax.numpy as jnp
import numpy as np
import ml_dtypes
from jax import lax
from jax.experimental import pallas as pl
from jax.experimental.pallas import tpu as pltpu
from jax.sharding import PartitionSpec as P

BATCHES = 3
STEP = 0.5
VMEM_LIMIT = 50 * 1024 * 1024


def shifted(array, axis, by):
    size = lax.axis_size(axis)
    pairs = [(i, i + by) for i in range(size) if 0 <= i + by < size]
    return lax.ppermute(array, axis, pairs)


def tables(length):
    index = np.arange(length)
    angle = (index[:, None] * index[None, :] % length) * (-2.0 * math.pi / length)
    scale = 1.0 / math.sqrt(length)
    re, im = np.cos(angle) * scale, np.sin(angle) * scale
    right = np.block([[re, im], [-im, re]]).astype(np.float32)
    high = right.astype(ml_dtypes.bfloat16)
    low = (right - high.astype(np.float32)).astype(ml_dtypes.bfloat16)
    stacked = np.concatenate([high, high, low], axis=0)
    return stacked, np.ascontiguousarray(stacked.T)


def split(value):
    high = value.astype(jnp.bfloat16)
    low = (value - high.astype(jnp.float32)).astype(jnp.bfloat16)
    return high, low


def forward(re, im, right_ref, left_ref):
    n = re.shape[0]
    (rh, rl), (ih, il) = split(re), split(im)
    y = jnp.dot(
        jnp.concatenate([rh, ih, rl, il, rh, ih], axis=1),
        right_ref[...],
        preferred_element_type=jnp.float32,
    )
    (rh, rl), (ih, il) = split(y[:, :n]), split(y[:, n:])
    z = jnp.dot(
        left_ref[...],
        jnp.concatenate([rh, ih, rl, il, rh, ih], axis=0),
        preferred_element_type=jnp.float32,
    )
    return z[:n], z[n:]


def inverse(re, im, right_ref, left_ref):
    out_im, out_re = forward(im, re, right_ref, left_ref)
    return out_re, out_im


def window_kernel(batch, first, last, *refs):
    count, row_off, col_off, which, keep = refs[:5]
    n_in = 4 if first else 8
    pieces = refs[5 : 5 + n_in]
    rest = refs[5 + n_in :]
    probe, prop, amplitude, right_t, left_t = rest[:5]
    rest = rest[5:]
    if last:
        base, down, right_one, right_two, ext, delta = rest
    else:
        base, down, up, right_one, left_one, ext, delta = rest
    win = probe.shape[1]
    strip = win // 2
    rows = ext.shape[2] - 8 - strip
    cols = ext.shape[3] - strip
    wide = cols + strip
    slots = amplitude.shape[0]

    if first:
        current, below, side, corner = pieces
        for a in range(2):
            for b in range(2):
                ext[a, b, :rows, :cols] = current[a, b]
                ext[a, b, rows : rows + strip, :cols] = below[a, b]
                ext[a, b, :rows, cols:] = side[a, b]
                ext[a, b, rows : rows + strip, cols:] = corner[a, b]
    else:
        old, from_up, from_down, fr_one, fr_two, fl_one, fl_two, corner = pieces
        keep_row = keep[0].astype(jnp.float32)
        keep_col = keep[1].astype(jnp.float32)
        for a in range(2):
            for b in range(2):
                ext[a, b, :strip, :strip] = old[a, b, :strip, :strip] + from_up[a, b, :, :strip] + fr_two[a, b]
                ext[a, b, :strip, strip:cols] = old[a, b, :strip, strip:cols] + from_up[a, b, :, strip:cols]
                ext[a, b, :strip, cols:] = (
                    old[a, b, :strip, cols:] + from_up[a, b, :, cols:] + fl_two[a, b]
                ) * keep_col
                ext[a, b, strip:rows, :strip] = old[a, b, strip:rows, :strip] + fr_one[a, b]
                ext[a, b, strip:rows, strip:cols] = old[a, b, strip:rows, strip:cols]
                ext[a, b, strip:rows, cols:] = (old[a, b, strip:rows, cols:] + fl_one[a, b]) * keep_col
                bottom = pl.ds(rows, strip)
                ext[a, b, bottom, :strip] = (
                    old[a, b, bottom, :strip] + from_down[a, b, :, :strip] + corner[a, b, :, :strip]
                ) * keep_row
                ext[a, b, bottom, strip:cols] = (
                    old[a, b, bottom, strip:cols] + from_down[a, b, :, strip:cols]
                ) * keep_row
                ext[a, b, bottom, cols:] = (
                    old[a, b, bottom, cols:] + from_down[a, b, :, cols:] + corner[a, b, :, strip:]
                ) * (keep_row * keep_col)
    for a in range(2):
        for b in range(2):
            delta[a, b] = jnp.zeros(delta.shape[2:], jnp.float32)

    def visit(slot, carry):
        @pl.when((slot < count[0, 0]) & (which[0, 0, slot] == batch))
        def _():
            top = row_off[0, 0, slot]
            shift_c = col_off[0, 0, slot]
            origin = pl.multiple_of((top // 8) * 8, 8)
            shift_r = top - origin
            tail = pl.multiple_of(origin + win, 8)
            in_tail = lax.broadcasted_iota(jnp.int32, (8, wide), 0) < shift_r
            in_side = lax.broadcasted_iota(jnp.int32, (win, strip), 1) < shift_c

            def window(a, b):
                head = jnp.where(in_tail, ext[a, b, pl.ds(tail, 8), :], ext[a, b, pl.ds(origin, 8), :])
                body = ext[a, b, pl.ds(origin + 8, win - 8), :]
                full = jnp.concatenate([head, body], axis=0)
                near = jnp.where(in_side, full[:, cols:], full[:, :strip])
                return jnp.concatenate([near, full[:, strip:cols]], axis=1)

            def add(a, b, value):
                value = value * (-STEP)
                near = value[:, :strip]
                zero = jnp.zeros_like(near)
                full = jnp.concatenate(
                    [jnp.where(in_side, zero, near), value[:, strip:], jnp.where(in_side, near, zero)], axis=1
                )
                head = full[:8]
                nothing = jnp.zeros_like(head)
                delta[a, b, pl.ds(origin, 8), :] += jnp.where(in_tail, nothing, head)
                delta[a, b, pl.ds(origin + 8, win - 8), :] += full[8:]
                delta[a, b, pl.ds(tail, 8), :] += jnp.where(in_tail, head, nothing)

            pr = pltpu.roll(pltpu.roll(probe[0], shift_c, 1), shift_r, 0)
            pi = pltpu.roll(pltpu.roll(probe[1], shift_c, 1), shift_r, 0)
            wr, wi = window(0, 0), window(0, 1)
            fr, fi = forward(pr * wr - pi * wi, pr * wi + pi * wr, right_t, left_t)
            hr, hi = prop[0], prop[1]
            br, bi = inverse(hr * fr - hi * fi, hr * fi + hi * fr, right_t, left_t)
            wr, wi = window(1, 0), window(1, 1)
            fr, fi = forward(br * wr - bi * wi, br * wi + bi * wr, right_t, left_t)
            factor = 1.0 - amplitude[slot] * lax.rsqrt(jnp.maximum(fr * fr + fi * fi, 1.0))
            gr, gi = inverse(fr * factor, fi * factor, right_t, left_t)
            add(1, 0, br * gr + bi * gi)
            add(1, 1, br * gi - bi * gr)
            fr, fi = forward(wr * gr + wi * gi, wr * gi - wi * gr, right_t, left_t)
            hr, hi = prop[0], prop[1]
            gr, gi = inverse(hr * fr + hi * fi, hr * fi - hi * fr, right_t, left_t)
            add(0, 0, pr * gr + pi * gi)
            add(0, 1, pr * gi - pi * gr)

        return carry

    lax.fori_loop(0, slots, visit, 0)
    for a in range(2):
        for b in range(2):
            if last:
                base[a, b] = ext[a, b, :rows, :cols] + delta[a, b, :rows, :cols]
                right_two[a, b] = delta[a, b, :strip, cols:]
            else:
                base[a, b] = ext[a, b, : rows + strip] + delta[a, b, : rows + strip]
                up[a, b] = delta[a, b, :strip]
                left_one[a, b] = delta[a, b, strip:rows, :strip]
            down[a, b] = delta[a, b, rows : rows + strip]
            right_one[a, b] = delta[a, b, strip:rows, cols:]


def finish_kernel(base, from_up, fr_one, fr_two, out):
    rows, cols = out.shape[2:]
    strip = from_up.shape[2]
    for a in range(2):
        for b in range(2):
            out[a, b, :strip, :strip] = base[a, b, :strip, :strip] + from_up[a, b, :, :strip] + fr_two[a, b]
            out[a, b, :strip, strip:] = base[a, b, :strip, strip:] + from_up[a, b, :, strip:cols]
            out[a, b, strip:, :strip] = base[a, b, strip:, :strip] + fr_one[a, b]
            out[a, b, strip:, strip:] = base[a, b, strip:, strip:]


def body(
    transmission, probe, prop_phase, amplitude, window_count, offset_row, offset_col, window_batch
):
    win = probe.shape[1]
    strip = win // 2
    rows, cols = transmission.shape[2:]
    wide = cols + strip
    right_t, left_t = (jnp.asarray(t) for t in tables(win))
    prop = jnp.stack([jnp.cos(prop_phase), jnp.sin(prop_phase)])
    measured = amplitude[0, 0]
    keep = jnp.stack(
        [
            (lax.axis_index("row") < lax.axis_size("row") - 1).astype(jnp.int32),
            (lax.axis_index("col") < lax.axis_size("col") - 1).astype(jnp.int32),
        ]
    )
    smem = pl.BlockSpec(memory_space=pltpu.SMEM)
    vmem = pl.BlockSpec(memory_space=pltpu.VMEM)

    def shape(r, c):
        return jax.ShapeDtypeStruct((2, 2, r, c), jnp.float32)

    def windows(batch, pieces):
        first, last = batch == 0, batch == BATCHES - 1
        if last:
            outs = (shape(rows, cols), shape(strip, wide), shape(rows - strip, strip), shape(strip, strip))
        else:
            outs = (
                shape(rows + strip, wide),
                shape(strip, wide),
                shape(strip, wide),
                shape(rows - strip, strip),
                shape(rows - strip, strip),
            )
        return pl.pallas_call(
            functools.partial(window_kernel, batch, first, last),
            out_shape=outs,
            in_specs=[smem] * 5 + [vmem] * (len(pieces) + 5),
            out_specs=[vmem] * len(outs),
            scratch_shapes=[
                pltpu.VMEM((2, 2, rows + strip + 8, wide), jnp.float32),
                pltpu.VMEM((2, 2, rows + strip + 8, wide), jnp.float32),
            ],
            compiler_params=pltpu.CompilerParams(vmem_limit_bytes=VMEM_LIMIT),
            name=f"windows{batch}",
        )(
            window_count, offset_row, offset_col, window_batch, keep, *pieces,
            probe, prop, measured, right_t, left_t,
        )

    side = shifted(transmission[:, :, :, :strip], "col", -1)
    below = shifted(transmission[:, :, :strip, :], "row", -1)
    corner = shifted(side[:, :, :strip, :], "row", -1)
    pieces = (transmission, below, side, corner)
    for batch in range(BATCHES - 1):
        base, down, up, right_one, left_one = windows(batch, pieces)
        from_up = shifted(down, "row", 1)
        from_down = shifted(up, "row", -1)
        fr_one = shifted(right_one, "col", 1)
        fl_one = shifted(left_one, "col", -1)
        fr_two = shifted(up[..., cols:] + from_up[..., cols:], "col", 1)
        fl_two = shifted(up[..., :strip] + from_up[..., :strip], "col", -1)
        corner = shifted(jnp.concatenate([fr_two, fl_two], axis=3), "row", -1)
        pieces = (base, from_up, from_down, fr_one, fr_two, fl_one, fl_two, corner)
    base, down, right_one, right_two = windows(BATCHES - 1, pieces)
    from_up = shifted(down, "row", 1)
    fr_one = shifted(right_one, "col", 1)
    fr_two = shifted(right_two + from_up[..., cols:], "col", 1)
    return pl.pallas_call(
        finish_kernel,
        out_shape=shape(rows, cols),
        in_specs=[vmem] * 4,
        out_specs=vmem,
        compiler_params=pltpu.CompilerParams(vmem_limit_bytes=VMEM_LIMIT),
        name="finish",
    )(base, from_up, fr_one, fr_two)


def solution(mesh):
    in_specs = (
        P(None, None, "row", "col"),
        P(),
        P(),
        P("row", "col", None, None, None),
        P("row", "col"),
        P("row", "col", None),
        P("row", "col", None),
        P("row", "col", None),
    )
    out_specs = P(None, None, "row", "col")
    return jax.shard_map(body, mesh=mesh, in_specs=in_specs, out_specs=out_specs, check_vma=False)
```

```python
import functools
import math

import jax
import jax.numpy as jnp
import numpy as np
import ml_dtypes
from jax import lax
from jax.experimental import pallas as pl
from jax.experimental.pallas import tpu as pltpu
from jax.sharding import PartitionSpec as P

BATCHES = 3
STEP = 0.5
VMEM_LIMIT = 32 * 1024 * 1024


def shifted(array, axis, by):
    size = lax.axis_size(axis)
    pairs = [(i, i + by) for i in range(size) if 0 <= i + by < size]
    return lax.ppermute(array, axis, pairs)


def tables(length):
    half = length // 2
    index = np.arange(half)
    scale = 1.0 / math.sqrt(length)
    lefts = []
    for odd in range(2):
        angle = ((2 * index[:, None] + odd) * index[None, :] % length) * (-2.0 * math.pi / length)
        re, im = np.cos(angle) * scale, np.sin(angle) * scale
        real = np.block([[re, -im], [im, re]]).astype(np.float32)
        lefts.append(real)
    out = []
    for real in lefts + [m.T for m in lefts]:
        high = real.astype(ml_dtypes.bfloat16)
        low = (real - high.astype(np.float32)).astype(ml_dtypes.bfloat16)
        out.append(np.concatenate([high, high, low], axis=1))
    left = np.stack(out)
    right = np.stack([np.concatenate([m[:, :length].T, m[:, length : 2 * length].T, m[:, 2 * length :].T]) for m in out])
    pick = np.zeros((length, length), np.float32)
    order = np.concatenate([np.arange(0, length, 2), np.arange(1, length, 2)])
    pick[np.arange(length), order] = 1.0
    pick = np.concatenate([pick] * 3, axis=1).astype(ml_dtypes.bfloat16)
    return left, right, pick, np.ascontiguousarray(pick.T)


def split(value):
    high = value.astype(jnp.bfloat16)
    low = (value - high.astype(jnp.float32)).astype(jnp.bfloat16)
    return high, low


def on_rows(table, value):
    high, low = split(value)
    return jnp.dot(table, jnp.concatenate([high, low, high], axis=0), preferred_element_type=jnp.float32)


def on_cols(value, table):
    high, low = split(value)
    return jnp.dot(jnp.concatenate([high, low, high], axis=1), table, preferred_element_type=jnp.float32)


def halves(value, axis):
    half = value.shape[axis] // 2
    return (value[:half], value[half:]) if axis == 0 else (value[:, :half], value[:, half:])


def forward_axis(re, im, axis, apply):
    (ra, rb), (ia, ib) = halves(re, axis), halves(im, axis)
    even = apply(0, jnp.concatenate([ra + rb, ia + ib], axis=axis))
    odd = apply(1, jnp.concatenate([ra - rb, ia - ib], axis=axis))
    (er, ei), (dr, di) = halves(even, axis), halves(odd, axis)
    return jnp.concatenate([er, dr], axis=axis), jnp.concatenate([ei, di], axis=axis)


def inverse_axis(re, im, axis, apply):
    (er, dr), (ei, di) = halves(re, axis), halves(im, axis)
    even = apply(2, jnp.concatenate([er, ei], axis=axis))
    odd = apply(3, jnp.concatenate([dr, di], axis=axis))
    (ra, ia), (rb, ib) = halves(even + odd, axis), halves(even - odd, axis)
    return jnp.concatenate([ra, rb], axis=axis), jnp.concatenate([ia, ib], axis=axis)


def forward(re, im, right_ref, left_ref):
    re, im = forward_axis(re, im, 1, lambda i, v: on_cols(v, right_ref[i]))
    return forward_axis(re, im, 0, lambda i, v: on_rows(left_ref[i], v))


def inverse(re, im, right_ref, left_ref):
    re, im = inverse_axis(re, im, 0, lambda i, v: on_rows(left_ref[i], v))
    return inverse_axis(re, im, 1, lambda i, v: on_cols(v, right_ref[i]))


def thirds(value):
    high = value.astype(jnp.bfloat16)
    value = value - high.astype(jnp.float32)
    middle = value.astype(jnp.bfloat16)
    low = (value - middle.astype(jnp.float32)).astype(jnp.bfloat16)
    return [high, middle, low]


def reorder_kernel(amplitude, prop, pick, pick_t, amplitude_out, prop_out):
    def move(value):
        rows = jnp.dot(pick[...], jnp.concatenate(thirds(value), axis=0), preferred_element_type=jnp.float32)
        return jnp.dot(jnp.concatenate(thirds(rows), axis=1), pick_t[...], preferred_element_type=jnp.float32)

    def each(source, target):
        def step(i, carry):
            target[i] = move(source[i])
            return carry

        lax.fori_loop(0, source.shape[0], step, 0)

    each(amplitude, amplitude_out)
    each(prop, prop_out)


def window_kernel(batch, first, last, *refs):
    count, row_off, col_off, which, keep = refs[:5]
    n_in = 4 if first else 8
    pieces = refs[5 : 5 + n_in]
    rest = refs[5 + n_in :]
    probe, prop, amplitude, right_t, left_t = rest[:5]
    rest = rest[5:]
    if last:
        base, down, right_one, right_two, ext, delta = rest
    else:
        base, down, up, right_one, left_one, ext, delta = rest
    win = probe.shape[1]
    strip = win // 2
    rows = ext.shape[2] - 8 - strip
    cols = ext.shape[3] - strip
    wide = cols + strip
    slots = amplitude.shape[0]

    if first:
        current, below, side, corner = pieces
        for a in range(2):
            for b in range(2):
                ext[a, b, :rows, :cols] = current[a, b]
                ext[a, b, rows : rows + strip, :cols] = below[a, b]
                ext[a, b, :rows, cols:] = side[a, b]
                ext[a, b, rows : rows + strip, cols:] = corner[a, b]
    else:
        old, from_up, from_down, fr_one, fr_two, fl_one, fl_two, corner = pieces
        keep_row = keep[0].astype(jnp.float32)
        keep_col = keep[1].astype(jnp.float32)
        for a in range(2):
            for b in range(2):
                ext[a, b, :strip, :strip] = old[a, b, :strip, :strip] + from_up[a, b, :, :strip] + fr_two[a, b]
                ext[a, b, :strip, strip:cols] = old[a, b, :strip, strip:cols] + from_up[a, b, :, strip:cols]
                ext[a, b, :strip, cols:] = (
                    old[a, b, :strip, cols:] + from_up[a, b, :, cols:] + fl_two[a, b]
                ) * keep_col
                ext[a, b, strip:rows, :strip] = old[a, b, strip:rows, :strip] + fr_one[a, b]
                ext[a, b, strip:rows, strip:cols] = old[a, b, strip:rows, strip:cols]
                ext[a, b, strip:rows, cols:] = (old[a, b, strip:rows, cols:] + fl_one[a, b]) * keep_col
                bottom = pl.ds(rows, strip)
                ext[a, b, bottom, :strip] = (
                    old[a, b, bottom, :strip] + from_down[a, b, :, :strip] + corner[a, b, :, :strip]
                ) * keep_row
                ext[a, b, bottom, strip:cols] = (
                    old[a, b, bottom, strip:cols] + from_down[a, b, :, strip:cols]
                ) * keep_row
                ext[a, b, bottom, cols:] = (
                    old[a, b, bottom, cols:] + from_down[a, b, :, cols:] + corner[a, b, :, strip:]
                ) * (keep_row * keep_col)
    for a in range(2):
        for b in range(2):
            delta[a, b] = jnp.zeros(delta.shape[2:], jnp.float32)

    def visit(slot, carry):
        @pl.when((slot < count[0, 0]) & (which[0, 0, slot] == batch))
        def _():
            top = row_off[0, 0, slot]
            shift_c = col_off[0, 0, slot]
            origin = pl.multiple_of((top // 8) * 8, 8)
            shift_r = top - origin
            tail = pl.multiple_of(origin + win, 8)
            in_tail = lax.broadcasted_iota(jnp.int32, (8, wide), 0) < shift_r
            in_side = lax.broadcasted_iota(jnp.int32, (win, strip), 1) < shift_c

            def window(a, b):
                head = jnp.where(in_tail, ext[a, b, pl.ds(tail, 8), :], ext[a, b, pl.ds(origin, 8), :])
                body = ext[a, b, pl.ds(origin + 8, win - 8), :]
                full = jnp.concatenate([head, body], axis=0)
                near = jnp.where(in_side, full[:, cols:], full[:, :strip])
                return jnp.concatenate([near, full[:, strip:cols]], axis=1)

            def add(a, b, value):
                value = value * (-STEP)
                near = value[:, :strip]
                zero = jnp.zeros_like(near)
                full = jnp.concatenate(
                    [jnp.where(in_side, zero, near), value[:, strip:], jnp.where(in_side, near, zero)], axis=1
                )
                head = full[:8]
                nothing = jnp.zeros_like(head)
                delta[a, b, pl.ds(origin, 8), :] += jnp.where(in_tail, nothing, head)
                delta[a, b, pl.ds(origin + 8, win - 8), :] += full[8:]
                delta[a, b, pl.ds(tail, 8), :] += jnp.where(in_tail, head, nothing)

            pr = pltpu.roll(pltpu.roll(probe[0], shift_c, 1), shift_r, 0)
            pi = pltpu.roll(pltpu.roll(probe[1], shift_c, 1), shift_r, 0)
            wr, wi = window(0, 0), window(0, 1)
            fr, fi = forward(pr * wr - pi * wi, pr * wi + pi * wr, right_t, left_t)
            hr, hi = prop[0], prop[1]
            br, bi = inverse(hr * fr - hi * fi, hr * fi + hi * fr, right_t, left_t)
            wr, wi = window(1, 0), window(1, 1)
            fr, fi = forward(br * wr - bi * wi, br * wi + bi * wr, right_t, left_t)
            factor = 1.0 - amplitude[slot] * lax.rsqrt(jnp.maximum(fr * fr + fi * fi, 1.0))
            gr, gi = inverse(fr * factor, fi * factor, right_t, left_t)
            add(1, 0, br * gr + bi * gi)
            add(1, 1, br * gi - bi * gr)
            fr, fi = forward(wr * gr + wi * gi, wr * gi - wi * gr, right_t, left_t)
            hr, hi = prop[0], prop[1]
            gr, gi = inverse(hr * fr + hi * fi, hr * fi - hi * fr, right_t, left_t)
            add(0, 0, pr * gr + pi * gi)
            add(0, 1, pr * gi - pi * gr)

        return carry

    lax.fori_loop(0, slots, visit, 0)
    for a in range(2):
        for b in range(2):
            if last:
                base[a, b] = ext[a, b, :rows, :cols] + delta[a, b, :rows, :cols]
                right_two[a, b] = delta[a, b, :strip, cols:]
            else:
                base[a, b] = ext[a, b, : rows + strip] + delta[a, b, : rows + strip]
                up[a, b] = delta[a, b, :strip]
                left_one[a, b] = delta[a, b, strip:rows, :strip]
            down[a, b] = delta[a, b, rows : rows + strip]
            right_one[a, b] = delta[a, b, strip:rows, cols:]


def finish_kernel(base, from_up, fr_one, fr_two, out):
    rows, cols = out.shape[2:]
    strip = from_up.shape[2]
    for a in range(2):
        for b in range(2):
            out[a, b, :strip, :strip] = base[a, b, :strip, :strip] + from_up[a, b, :, :strip] + fr_two[a, b]
            out[a, b, :strip, strip:] = base[a, b, :strip, strip:] + from_up[a, b, :, strip:cols]
            out[a, b, strip:, :strip] = base[a, b, strip:, :strip] + fr_one[a, b]
            out[a, b, strip:, strip:] = base[a, b, strip:, strip:]


def body(
    transmission, probe, prop_phase, amplitude, window_count, offset_row, offset_col, window_batch
):
    win = probe.shape[1]
    strip = win // 2
    rows, cols = transmission.shape[2:]
    wide = cols + strip
    left_t, right_t, pick, pick_t = (jnp.asarray(t) for t in tables(win))
    prop = jnp.stack([jnp.cos(prop_phase), jnp.sin(prop_phase)])
    measured = amplitude[0, 0]
    keep = jnp.stack(
        [
            (lax.axis_index("row") < lax.axis_size("row") - 1).astype(jnp.int32),
            (lax.axis_index("col") < lax.axis_size("col") - 1).astype(jnp.int32),
        ]
    )
    smem = pl.BlockSpec(memory_space=pltpu.SMEM)
    vmem = pl.BlockSpec(memory_space=pltpu.VMEM)
    planes = amplitude.shape[2] + 2
    measured, prop = pl.pallas_call(
        reorder_kernel,
        out_shape=(
            jax.ShapeDtypeStruct(measured.shape, jnp.float32),
            jax.ShapeDtypeStruct(prop.shape, jnp.float32),
        ),
        in_specs=[vmem] * 4,
        out_specs=(vmem, vmem),
        compiler_params=pltpu.CompilerParams(vmem_limit_bytes=VMEM_LIMIT // 2),
        cost_estimate=pl.CostEstimate(
            flops=planes * 12 * win**3, bytes_accessed=planes * 8 * win**2, transcendentals=0
        ),
        name="reorder",
    )(measured, prop, pick, pick_t)

    def shape(r, c):
        return jax.ShapeDtypeStruct((2, 2, r, c), jnp.float32)

    def windows(batch, pieces):
        first, last = batch == 0, batch == BATCHES - 1
        if last:
            outs = (shape(rows, cols), shape(strip, wide), shape(rows - strip, strip), shape(strip, strip))
        else:
            outs = (
                shape(rows + strip, wide),
                shape(strip, wide),
                shape(strip, wide),
                shape(rows - strip, strip),
                shape(rows - strip, strip),
            )
        return pl.pallas_call(
            functools.partial(window_kernel, batch, first, last),
            out_shape=outs,
            in_specs=[smem] * 5 + [vmem] * (len(pieces) + 5),
            out_specs=[vmem] * len(outs),
            scratch_shapes=[
                pltpu.VMEM((2, 2, rows + strip + 8, wide), jnp.float32),
                pltpu.VMEM((2, 2, rows + strip + 8, wide), jnp.float32),
            ],
            compiler_params=pltpu.CompilerParams(vmem_limit_bytes=VMEM_LIMIT),
            name=f"windows{batch}",
        )(
            window_count, offset_row, offset_col, window_batch, keep, *pieces,
            probe, prop, measured, right_t, left_t,
        )

    side = shifted(transmission[:, :, :, :strip], "col", -1)
    below = shifted(transmission[:, :, :strip, :], "row", -1)
    corner = shifted(side[:, :, :strip, :], "row", -1)
    pieces = (transmission, below, side, corner)
    for batch in range(BATCHES - 1):
        base, down, up, right_one, left_one = windows(batch, pieces)
        from_up = shifted(down, "row", 1)
        from_down = shifted(up, "row", -1)
        fr_one = shifted(right_one, "col", 1)
        fl_one = shifted(left_one, "col", -1)
        fr_two = shifted(up[..., cols:] + from_up[..., cols:], "col", 1)
        fl_two = shifted(up[..., :strip] + from_up[..., :strip], "col", -1)
        corner = shifted(jnp.concatenate([fr_two, fl_two], axis=3), "row", -1)
        pieces = (base, from_up, from_down, fr_one, fr_two, fl_one, fl_two, corner)
    base, down, right_one, right_two = windows(BATCHES - 1, pieces)
    from_up = shifted(down, "row", 1)
    fr_one = shifted(right_one, "col", 1)
    fr_two = shifted(right_two + from_up[..., cols:], "col", 1)
    return pl.pallas_call(
        finish_kernel,
        out_shape=shape(rows, cols),
        in_specs=[vmem] * 4,
        out_specs=vmem,
        compiler_params=pltpu.CompilerParams(vmem_limit_bytes=VMEM_LIMIT),
        name="finish",
    )(base, from_up, fr_one, fr_two)


def solution(mesh):
    in_specs = (
        P(None, None, "row", "col"),
        P(),
        P(),
        P("row", "col", None, None, None),
        P("row", "col"),
        P("row", "col", None),
        P("row", "col", None),
        P("row", "col", None),
    )
    out_specs = P(None, None, "row", "col")
    return jax.shard_map(body, mesh=mesh, in_specs=in_specs, out_specs=out_specs, check_vma=False)
```

```python
import functools
import math

import jax
import jax.numpy as jnp
import numpy as np
import ml_dtypes
from jax import lax
from jax.experimental import pallas as pl
from jax.experimental.pallas import tpu as pltpu
from jax.sharding import PartitionSpec as P

BATCHES = 3
STEP = 0.5
VMEM_LIMIT = 32 * 1024 * 1024


def shifted(array, axis, by):
    size = lax.axis_size(axis)
    pairs = [(i, i + by) for i in range(size) if 0 <= i + by < size]
    return lax.ppermute(array, axis, pairs)


def tables(length):
    half = length // 2
    index = np.arange(half)
    scale = 1.0 / math.sqrt(length)
    lefts = []
    for odd in range(2):
        angle = ((2 * index[:, None] + odd) * index[None, :] % length) * (-2.0 * math.pi / length)
        re, im = np.cos(angle) * scale, np.sin(angle) * scale
        real = np.block([[re, -im], [im, re]]).astype(np.float32)
        lefts.append(real)
    out = []
    for real in lefts + [m.T for m in lefts]:
        high = real.astype(ml_dtypes.bfloat16)
        low = (real - high.astype(np.float32)).astype(ml_dtypes.bfloat16)
        out.append(np.concatenate([high, high, low], axis=1))
    left = np.stack(out)
    right = np.stack([np.concatenate([m[:, :length].T, m[:, length : 2 * length].T, m[:, 2 * length :].T]) for m in out])
    pick = np.zeros((length, length), np.float32)
    order = np.concatenate([np.arange(0, length, 2), np.arange(1, length, 2)])
    pick[np.arange(length), order] = 1.0
    pick = np.concatenate([pick] * 3, axis=1).astype(ml_dtypes.bfloat16)
    return left, right, pick, np.ascontiguousarray(pick.T)


def split(value):
    high = value.astype(jnp.bfloat16)
    low = (value - high.astype(jnp.float32)).astype(jnp.bfloat16)
    return high, low


def on_rows(table, value):
    high, low = split(value)
    return jnp.dot(table, jnp.concatenate([high, low, high], axis=0), preferred_element_type=jnp.float32)


def on_cols(value, table):
    high, low = split(value)
    return jnp.dot(jnp.concatenate([high, low, high], axis=1), table, preferred_element_type=jnp.float32)


def halves(value, axis):
    half = value.shape[axis] // 2
    return (value[:half], value[half:]) if axis == 0 else (value[:, :half], value[:, half:])


def forward_axis(re, im, axis, apply):
    (ra, rb), (ia, ib) = halves(re, axis), halves(im, axis)
    even = apply(0, jnp.concatenate([ra + rb, ia + ib], axis=axis))
    odd = apply(1, jnp.concatenate([ra - rb, ia - ib], axis=axis))
    (er, ei), (dr, di) = halves(even, axis), halves(odd, axis)
    return jnp.concatenate([er, dr], axis=axis), jnp.concatenate([ei, di], axis=axis)


def inverse_axis(re, im, axis, apply):
    (er, dr), (ei, di) = halves(re, axis), halves(im, axis)
    even = apply(2, jnp.concatenate([er, ei], axis=axis))
    odd = apply(3, jnp.concatenate([dr, di], axis=axis))
    (ra, ia), (rb, ib) = halves(even + odd, axis), halves(even - odd, axis)
    return jnp.concatenate([ra, rb], axis=axis), jnp.concatenate([ia, ib], axis=axis)


def forward(re, im, right_ref, left_ref):
    re, im = forward_axis(re, im, 1, lambda i, v: on_cols(v, right_ref[i]))
    return forward_axis(re, im, 0, lambda i, v: on_rows(left_ref[i], v))


def inverse(re, im, right_ref, left_ref):
    re, im = inverse_axis(re, im, 0, lambda i, v: on_rows(left_ref[i], v))
    return inverse_axis(re, im, 1, lambda i, v: on_cols(v, right_ref[i]))


def thirds(value):
    high = value.astype(jnp.bfloat16)
    value = value - high.astype(jnp.float32)
    middle = value.astype(jnp.bfloat16)
    low = (value - middle.astype(jnp.float32)).astype(jnp.bfloat16)
    return [high, middle, low]


def reorder_kernel(amplitude, prop, pick, pick_t, amplitude_out, prop_out):
    def move(value):
        rows = jnp.dot(pick[...], jnp.concatenate(thirds(value), axis=0), preferred_element_type=jnp.float32)
        return jnp.dot(jnp.concatenate(thirds(rows), axis=1), pick_t[...], preferred_element_type=jnp.float32)

    def each(source, target):
        def step(i, carry):
            target[i] = move(source[i])
            return carry

        lax.fori_loop(0, source.shape[0], step, 0)

    each(amplitude, amplitude_out)
    each(prop, prop_out)


def window_kernel(batch, first, last, *refs):
    count, row_off, col_off, which, keep = refs[:5]
    n_in = 5 if first else 9
    pieces = refs[5 : 5 + n_in]
    rest = refs[5 + n_in :]
    probe, prop, amplitude, right_t, left_t = rest[:5]
    rest = rest[5:]
    if last:
        base, down, right_one, right_two, ext, delta = rest
    else:
        base, down, up, right_one, left_one, ext, delta = rest
    win = probe.shape[1]
    strip = win // 2
    rows = ext.shape[2] - 8 - strip
    cols = ext.shape[3] - strip
    wide = cols + strip
    slots = amplitude.shape[0]

    if first:
        current, below, side_top, side_rest, corner = pieces
        for a in range(2):
            for b in range(2):
                ext[a, b, :rows, :cols] = current[a, b]
                ext[a, b, rows : rows + strip, :cols] = below[a, b]
                ext[a, b, :strip, cols:] = side_top[a, b]
                ext[a, b, strip:rows, cols:] = side_rest[a, b]
                ext[a, b, rows : rows + strip, cols:] = corner[a, b]
    else:
        old, from_up, from_down, fr_one, fr_two, fl_one, fl_two, corner_near, corner_far = pieces
        keep_row = keep[0].astype(jnp.float32)
        keep_col = keep[1].astype(jnp.float32)
        for a in range(2):
            for b in range(2):
                ext[a, b, :strip, :strip] = old[a, b, :strip, :strip] + from_up[a, b, :, :strip] + fr_two[a, b]
                ext[a, b, :strip, strip:cols] = old[a, b, :strip, strip:cols] + from_up[a, b, :, strip:cols]
                ext[a, b, :strip, cols:] = (
                    old[a, b, :strip, cols:] + from_up[a, b, :, cols:] + fl_two[a, b]
                ) * keep_col
                ext[a, b, strip:rows, :strip] = old[a, b, strip:rows, :strip] + fr_one[a, b]
                ext[a, b, strip:rows, strip:cols] = old[a, b, strip:rows, strip:cols]
                ext[a, b, strip:rows, cols:] = (old[a, b, strip:rows, cols:] + fl_one[a, b]) * keep_col
                bottom = pl.ds(rows, strip)
                ext[a, b, bottom, :strip] = (
                    old[a, b, bottom, :strip] + from_down[a, b, :, :strip] + corner_near[a, b]
                ) * keep_row
                ext[a, b, bottom, strip:cols] = (
                    old[a, b, bottom, strip:cols] + from_down[a, b, :, strip:cols]
                ) * keep_row
                ext[a, b, bottom, cols:] = (
                    old[a, b, bottom, cols:] + from_down[a, b, :, cols:] + corner_far[a, b]
                ) * (keep_row * keep_col)
    for a in range(2):
        for b in range(2):
            delta[a, b] = jnp.zeros(delta.shape[2:], jnp.float32)

    def visit(slot, carry):
        @pl.when((slot < count[0, 0]) & (which[0, 0, slot] == batch))
        def _():
            top = row_off[0, 0, slot]
            shift_c = col_off[0, 0, slot]
            origin = pl.multiple_of((top // 8) * 8, 8)
            shift_r = top - origin
            tail = pl.multiple_of(origin + win, 8)
            in_tail = lax.broadcasted_iota(jnp.int32, (8, wide), 0) < shift_r
            in_side = lax.broadcasted_iota(jnp.int32, (win, strip), 1) < shift_c

            def window(a, b):
                head = jnp.where(in_tail, ext[a, b, pl.ds(tail, 8), :], ext[a, b, pl.ds(origin, 8), :])
                body = ext[a, b, pl.ds(origin + 8, win - 8), :]
                full = jnp.concatenate([head, body], axis=0)
                near = jnp.where(in_side, full[:, cols:], full[:, :strip])
                return jnp.concatenate([near, full[:, strip:cols]], axis=1)

            def add(a, b, value):
                value = value * (-STEP)
                near = value[:, :strip]
                zero = jnp.zeros_like(near)
                full = jnp.concatenate(
                    [jnp.where(in_side, zero, near), value[:, strip:], jnp.where(in_side, near, zero)], axis=1
                )
                head = full[:8]
                nothing = jnp.zeros_like(head)
                delta[a, b, pl.ds(origin, 8), :] += jnp.where(in_tail, nothing, head)
                delta[a, b, pl.ds(origin + 8, win - 8), :] += full[8:]
                delta[a, b, pl.ds(tail, 8), :] += jnp.where(in_tail, head, nothing)

            pr = pltpu.roll(pltpu.roll(probe[0], shift_c, 1), shift_r, 0)
            pi = pltpu.roll(pltpu.roll(probe[1], shift_c, 1), shift_r, 0)
            wr, wi = window(0, 0), window(0, 1)
            fr, fi = forward(pr * wr - pi * wi, pr * wi + pi * wr, right_t, left_t)
            hr, hi = prop[0], prop[1]
            br, bi = inverse(hr * fr - hi * fi, hr * fi + hi * fr, right_t, left_t)
            wr, wi = window(1, 0), window(1, 1)
            fr, fi = forward(br * wr - bi * wi, br * wi + bi * wr, right_t, left_t)
            factor = 1.0 - amplitude[slot] * lax.rsqrt(jnp.maximum(fr * fr + fi * fi, 1.0))
            gr, gi = inverse(fr * factor, fi * factor, right_t, left_t)
            add(1, 0, br * gr + bi * gi)
            add(1, 1, br * gi - bi * gr)
            fr, fi = forward(wr * gr + wi * gi, wr * gi - wi * gr, right_t, left_t)
            hr, hi = prop[0], prop[1]
            gr, gi = inverse(hr * fr + hi * fi, hr * fi - hi * fr, right_t, left_t)
            add(0, 0, pr * gr + pi * gi)
            add(0, 1, pr * gi - pi * gr)

        return carry

    lax.fori_loop(0, slots, visit, 0)
    for a in range(2):
        for b in range(2):
            if last:
                base[a, b] = ext[a, b, :rows, :cols] + delta[a, b, :rows, :cols]
                right_two[a, b] = delta[a, b, :strip, cols:]
            else:
                base[a, b] = ext[a, b, : rows + strip] + delta[a, b, : rows + strip]
                up[a, b] = delta[a, b, :strip]
                left_one[a, b] = delta[a, b, strip:rows, :strip]
            down[a, b] = delta[a, b, rows : rows + strip]
            right_one[a, b] = delta[a, b, strip:rows, cols:]


def exchange_kernel(last, *refs):
    if last:
        down, right_one, right_two, from_up, fr_one, fr_two, send_right, send, recv = refs
        strip = right_two.shape[3]
    else:
        down, up, right_one, left_one = refs[:4]
        from_up, from_down, fr_one, fr_two, fl_one, fl_two, corner_near, corner_far = refs[4:12]
        send_right, send_left, send, recv = refs[12:]
        strip = right_one.shape[3]
    cols = down.shape[3] - strip
    row, col = lax.axis_index("row"), lax.axis_index("col")
    has_up, has_down = row > 0, row < lax.axis_size("row") - 1
    has_left, has_right = col > 0, col < lax.axis_size("col") - 1
    to_up, to_down, to_left, to_right = (row - 1, col), (row + 1, col), (row, col - 1), (row, col + 1)

    def copy(index, source, target, device):
        return pltpu.make_async_remote_copy(
            src_ref=source,
            dst_ref=target,
            send_sem=send.at[index],
            recv_sem=recv.at[index],
            device_id=device,
            device_id_type=pl.DeviceIdType.MESH,
        )

    copies = [
        (copy(0, right_one, fr_one, to_right), has_right, has_left, fr_one),
        (copy(1, down, from_up, to_down), has_down, has_up, from_up),
        (copy(2, send_right, fr_two, to_right), has_right, has_left, fr_two),
    ]
    if not last:
        copies += [
            (copy(3, left_one, fl_one, to_left), has_left, has_right, fl_one),
            (copy(4, up, from_down, to_up), has_up, has_down, from_down),
            (copy(5, send_left, fl_two, to_left), has_left, has_right, fl_two),
            (copy(6, fr_two, corner_near, to_up), has_up, has_down, corner_near),
            (copy(7, fl_two, corner_far, to_up), has_up, has_down, corner_far),
        ]

    def start(index):
        @pl.when(copies[index][1])
        def _():
            copies[index][0].start()

    def arrive(index):
        @pl.when(copies[index][2])
        def _():
            copies[index][0].wait_recv()

    for _, _, comes, target in copies:

        @pl.when(jnp.logical_not(comes))
        def _(target=target):
            target[...] = jnp.zeros(target.shape, jnp.float32)

    barrier = pltpu.get_barrier_semaphore()
    sides = ((has_up, to_up), (has_down, to_down), (has_left, to_left), (has_right, to_right))
    for there, device in sides:

        @pl.when(there)
        def _(device=device):
            pl.semaphore_signal(barrier, inc=1, device_id=device, device_id_type=pl.DeviceIdType.MESH)

    pl.semaphore_wait(barrier, sum(there.astype(jnp.int32) for there, _ in sides))

    start(1)
    start(0)
    if not last:
        start(3)
        start(4)
    arrive(1)
    if last:
        send_right[...] = right_two[...] + from_up[:, :, :, cols:]
        start(2)
        arrive(2)
    else:
        send_right[...] = up[:, :, :, cols:] + from_up[:, :, :, cols:]
        send_left[...] = up[:, :, :, :strip] + from_up[:, :, :, :strip]
        start(2)
        start(5)
        arrive(2)
        start(6)
        arrive(5)
        start(7)
        arrive(3)
        arrive(4)
        arrive(6)
        arrive(7)
    arrive(0)
    for one, goes, _, _ in copies:

        @pl.when(goes)
        def _(one=one):
            one.wait_send()


def finish_kernel(base, from_up, fr_one, fr_two, out):
    rows, cols = out.shape[2:]
    strip = from_up.shape[2]
    for a in range(2):
        for b in range(2):
            out[a, b, :strip, :strip] = base[a, b, :strip, :strip] + from_up[a, b, :, :strip] + fr_two[a, b]
            out[a, b, :strip, strip:] = base[a, b, :strip, strip:] + from_up[a, b, :, strip:cols]
            out[a, b, strip:, :strip] = base[a, b, strip:, :strip] + fr_one[a, b]
            out[a, b, strip:, strip:] = base[a, b, strip:, strip:]


def body(
    transmission, probe, prop_phase, amplitude, window_count, offset_row, offset_col, window_batch
):
    win = probe.shape[1]
    strip = win // 2
    rows, cols = transmission.shape[2:]
    wide = cols + strip
    left_t, right_t, pick, pick_t = (jnp.asarray(t) for t in tables(win))
    prop = jnp.stack([jnp.cos(prop_phase), jnp.sin(prop_phase)])
    measured = amplitude[0, 0]
    keep = jnp.stack(
        [
            (lax.axis_index("row") < lax.axis_size("row") - 1).astype(jnp.int32),
            (lax.axis_index("col") < lax.axis_size("col") - 1).astype(jnp.int32),
        ]
    )
    smem = pl.BlockSpec(memory_space=pltpu.SMEM)
    vmem = pl.BlockSpec(memory_space=pltpu.VMEM)
    planes = amplitude.shape[2] + 2
    measured, prop = pl.pallas_call(
        reorder_kernel,
        out_shape=(
            jax.ShapeDtypeStruct(measured.shape, jnp.float32),
            jax.ShapeDtypeStruct(prop.shape, jnp.float32),
        ),
        in_specs=[vmem] * 4,
        out_specs=(vmem, vmem),
        compiler_params=pltpu.CompilerParams(vmem_limit_bytes=VMEM_LIMIT // 2),
        cost_estimate=pl.CostEstimate(
            flops=planes * 12 * win**3, bytes_accessed=planes * 8 * win**2, transcendentals=0
        ),
        name="reorder",
    )(measured, prop, pick, pick_t)

    def shape(r, c):
        return jax.ShapeDtypeStruct((2, 2, r, c), jnp.float32)

    def windows(batch, pieces):
        first, last = batch == 0, batch == BATCHES - 1
        if last:
            outs = (shape(rows, cols), shape(strip, wide), shape(rows - strip, strip), shape(strip, strip))
        else:
            outs = (
                shape(rows + strip, wide),
                shape(strip, wide),
                shape(strip, wide),
                shape(rows - strip, strip),
                shape(rows - strip, strip),
            )
        return pl.pallas_call(
            functools.partial(window_kernel, batch, first, last),
            out_shape=outs,
            in_specs=[smem] * 5 + [vmem] * (len(pieces) + 5),
            out_specs=[vmem] * len(outs),
            scratch_shapes=[
                pltpu.VMEM((2, 2, rows + strip + 8, wide), jnp.float32),
                pltpu.VMEM((2, 2, rows + strip + 8, wide), jnp.float32),
            ],
            compiler_params=pltpu.CompilerParams(vmem_limit_bytes=VMEM_LIMIT),
            name=f"windows{batch}",
        )(
            window_count, offset_row, offset_col, window_batch, keep, *pieces,
            probe, prop, measured, right_t, left_t,
        )

    def exchange(batch, pieces):
        last = batch == BATCHES - 1
        block, rest = shape(strip, strip), shape(rows - strip, strip)
        if last:
            outs = (shape(strip, wide), rest, block)
        else:
            outs = (shape(strip, wide), shape(strip, wide), rest, block, rest, block, block, block)
        sends, copies = (1, 3) if last else (2, 8)
        return pl.pallas_call(
            functools.partial(exchange_kernel, last),
            out_shape=outs,
            in_specs=[vmem] * len(pieces),
            out_specs=[vmem] * len(outs),
            scratch_shapes=[pltpu.VMEM(block.shape, jnp.float32)] * sends
            + [pltpu.SemaphoreType.DMA((copies,)), pltpu.SemaphoreType.DMA((copies,))],
            compiler_params=pltpu.CompilerParams(
                vmem_limit_bytes=VMEM_LIMIT // 2, collective_id=batch, has_side_effects=True
            ),
            name=f"exchange{batch}",
        )(*pieces)

    side_top = shifted(transmission[:, :, :strip, :strip], "col", -1)
    side_rest = shifted(transmission[:, :, strip:, :strip], "col", -1)
    below = shifted(transmission[:, :, :strip, :], "row", -1)
    corner = shifted(side_top, "row", -1)
    pieces = (transmission, below, side_top, side_rest, corner)
    for batch in range(BATCHES - 1):
        base, *sent = windows(batch, pieces)
        pieces = (base, *exchange(batch, sent))
    base, *sent = windows(BATCHES - 1, pieces)
    from_up, fr_one, fr_two = exchange(BATCHES - 1, sent)
    return pl.pallas_call(
        finish_kernel,
        out_shape=shape(rows, cols),
        in_specs=[vmem] * 4,
        out_specs=vmem,
        compiler_params=pltpu.CompilerParams(vmem_limit_bytes=VMEM_LIMIT),
        name="finish",
    )(base, from_up, fr_one, fr_two)


def solution(mesh):
    in_specs = (
        P(None, None, "row", "col"),
        P(),
        P(),
        P("row", "col", None, None, None),
        P("row", "col"),
        P("row", "col", None),
        P("row", "col", None),
        P("row", "col", None),
    )
    out_specs = P(None, None, "row", "col")
    return jax.shard_map(body, mesh=mesh, in_specs=in_specs, out_specs=out_specs, check_vma=False)
```
